1024 devices in a mesh: row: 32 (over y, z_hi, core), col: 32 (over z_lo, x).
Axes of the slice: x: 4, y: 4, z: 32 (z_hi: 4, z_lo: 8; z = z_hi * 8 + z_lo), core: 2. Of those that a mesh axis runs over, the one named last changes fastest.
Arguments:
- a_blocks: bfloat16 [32, 32, 12, 128, 128], P('row', 'col'), may hold values from -6 to 6
- a_index: int32 [32, 32, 2, 12], P('row', 'col'), may hold values from 0 to 31, as said below
- a_count: int32 [32, 32], P('row', 'col'), may hold values from 6 to 12, as said below
- b_blocks: bfloat16 [1, 32, 32, 6, 128, 128], P(None, 'row', 'col'), may hold values from -0.5 to 0.5
- b_index: int32 [1, 32, 32, 2, 6], P(None, 'row', 'col'), may hold values from 0 to 31, as said below
- b_count: int32 [1, 32, 32], P(None, 'row', 'col'), may hold values from 3 to 6, as said below
Outputs:
- product: bfloat16 [32768, 16384], P('row', 'col')
The draws below stay inside these ranges and needn't reach their ends.
Inputs may be any that keep to these rules, and one draw needn't show every extreme that they name: Within one panel the stored positions are distinct; a_index rows are below 8 and columns below 32. Within one panel the stored positions are distinct; b_index rows are below 32 and columns below 4. `a_count`: slots at or past the count are padding. `b_count`: slots at or past the count are padding.
All inputs are finite; a program needn't handle non-finite values.
Results may differ from the reference program's by a relative error of at most 0.001.
Values may be sent and summed in bfloat16 or wider, within the bound.
No kernel may reach another device: no remote copies, remote signals or barrier semaphores. Data moves between devices by JAX's collectives and lax.ppermute only.
A program may use at most 32 MiB of HBM per device.

```python
import jax
import jax.numpy as jnp
from jax import lax

BLOCK = 128
KB = 32
KR = 8
KC = 4
TICKS = 4
SA = 12
SB = 6
GRID_ROWS = 32
GRID_COLS = 32
REPS = 1
CROWS = 32768
CCOLS = 16384


def index_pairs(key, panels, span, keep, width):
    keys = jax.random.split(key, panels)
    picks = jax.vmap(lambda one_key: jax.random.permutation(one_key, span)[:keep])(keys)
    return jnp.stack([picks // width, picks % width], axis=1).astype(jnp.int32)


def draw_a_index(key, part):
    key = jax.random.fold_in(key, 11)
    pairs = index_pairs(key, GRID_ROWS * GRID_COLS, KR * KB, SA, KB)
    return pairs.reshape(GRID_ROWS, GRID_COLS, 2, SA)


def draw_b_index(key, part):
    key = jax.random.fold_in(key, 12)
    pairs = index_pairs(key, REPS * GRID_ROWS * GRID_COLS, KB * KC, SB, KC)
    return pairs.reshape(REPS, GRID_ROWS, GRID_COLS, 2, SB)


def draw_a_count(key, part):
    key = jax.random.fold_in(key, 13)
    counts = jax.random.randint(key, (GRID_ROWS, GRID_COLS), SA // 2, SA + 1, dtype=jnp.int32)
    return counts.at[0, 0].set(SA)


def draw_b_count(key, part):
    key = jax.random.fold_in(key, 14)
    counts = jax.random.randint(key, (REPS, GRID_ROWS, GRID_COLS), SB // 2, SB + 1, dtype=jnp.int32)
    return counts.at[0, 0, 0].set(SB)


def levels(key, shape, shards, smallest, largest):
    level, own = 1.0, jax.random.fold_in(key, 6)
    for axis_at, shards_of in shards:
        steps = jnp.exp(jax.random.uniform(jax.random.fold_in(own, axis_at), (shards_of,), jnp.float32, smallest / len(shards), largest / len(shards)))
        level = level * jnp.repeat(steps, shape[axis_at] // shards_of).reshape([-1 if axis == axis_at else 1 for axis in range(len(shape))])
    return level


def gaussian(key, extent, deviation, bound, cuts=(), held_as=jnp.bfloat16):
    array = jax.random.normal(key, extent, jnp.float32) * deviation
    if len(cuts) > 0:
        array = levels(key, extent, cuts, -0.22, 0.18) * array
    return jnp.clip(array, min=-bound, max=bound).astype(held_as)


def setup_inputs(seed: int = 0) -> dict:
    key_list = jax.random.split(jax.random.key(seed), 7)
    return {
        "a_blocks": gaussian(key_list[0], (GRID_ROWS, GRID_COLS, SA, BLOCK, BLOCK), 1.0, 6.0, ((0, 32), (1, 32))),
        "a_index": draw_a_index(jax.random.fold_in(key_list[6], 71), 0),
        "a_count": draw_a_count(jax.random.fold_in(key_list[6], 71), 0),
        "b_blocks": gaussian(key_list[3], (REPS, GRID_ROWS, GRID_COLS, SB, BLOCK, BLOCK), BLOCK ** -0.5, 0.5, ((1, 32), (2, 32))),
        "b_index": draw_b_index(jax.random.fold_in(key_list[6], 71), 0),
        "b_count": draw_b_count(jax.random.fold_in(key_list[6], 71), 0),
    }


def panel_product(a_blk, a_idx, a_cnt, b_blk, b_idx, b_cnt):
    slots_a = a_blk.shape[0]
    slots_b = b_blk.shape[0]
    side = a_blk.shape[-1]
    live_a = jnp.arange(slots_a, dtype=jnp.int32) < a_cnt
    live_b = jnp.arange(slots_b, dtype=jnp.int32) < b_cnt
    match = (a_idx[1][:, None] == b_idx[0][None, :]) & live_a[:, None] & live_b[None, :]
    place = b_idx[1][:, None] == jnp.arange(KC, dtype=jnp.int32)[None, :]
    select = (match[:, :, None] & place[None, :, :]).astype(jnp.float32)
    strip = jnp.einsum("suc,uxy->sxcy", select, b_blk.astype(jnp.float32), precision=lax.Precision.HIGHEST)
    strip = strip.astype(jnp.bfloat16).astype(jnp.float32).reshape(slots_a, side, KC * side)
    prods = jnp.einsum("sxy,syz->sxz", a_blk.astype(jnp.float32), strip, precision=lax.Precision.HIGHEST)
    rowhot = ((a_idx[0][:, None] == jnp.arange(KR, dtype=jnp.int32)[None, :]) & live_a[:, None]).astype(jnp.float32)
    result = jnp.einsum("sr,sxz->rxz", rowhot, prods, precision=lax.Precision.HIGHEST)
    return result.reshape(KR * side, KC * side)


def reference(a_blocks, a_index, a_count, b_blocks, b_index, b_count):
    def one_panel(panel):
        i = panel // GRID_COLS
        j = panel % GRID_COLS
        total = jnp.zeros((KR * BLOCK, KC * BLOCK), jnp.float32)
        for tick in range(TICKS):
            inner = (i + j + tick) % GRID_COLS
            slot = inner // GRID_ROWS
            owner = inner % GRID_ROWS
            total = total + panel_product(a_blocks[i, inner], a_index[i, inner], a_count[i, inner],
                                          b_blocks[slot, owner, j], b_index[slot, owner, j], b_count[slot, owner, j])
        return total.astype(jnp.bfloat16)

    panels = jnp.arange(GRID_ROWS * GRID_COLS, dtype=jnp.int32)
    result = lax.map(one_panel, panels, batch_size=8)
    result = result.reshape(GRID_ROWS, GRID_COLS, KR * BLOCK, KC * BLOCK)
    return result.transpose(0, 2, 1, 3).reshape(CROWS, CCOLS)
```

```python
import jax
import jax.numpy as jnp
import numpy as np
from jax import lax
from jax.experimental import pallas as pl
from jax.experimental.pallas import tpu as pltpu
from jax.sharding import PartitionSpec as P

BLOCK = 128
KR = 8
KC = 4
TICKS = 4
SA = 12
SB = 6
GRID = 32
CHIPS = GRID // 2
TAG = 16
AXES = ("row", "col")

ROLES = {
    (0, 0): {"first": "F", "near": "O", "relay": "H"},
    (0, 1): {"first": "O", "near": "H", "relay": "F"},
    (0, 2): {"first": "F", "near": "H", "relay": "O"},
    (0, 3): {"first": "O", "near": "F", "last": "H"},
    (1, 0): {"first": "F", "near": "H", "relay": "O"},
    (1, 1): {"first": "O", "near": "H", "relay": "F"},
    (1, 2): {"first": "F", "near": "O", "relay": "H"},
    (1, 3): {"first": "O", "near": "F", "last": "H"},
}
MOVES = ("first", "near", "last", "relay")
SWAPS = ("first", "near", "relay")


def offset_of(role, p):
    return {"F": 1, "O": 2 * p, "H": 2 - 2 * p}[role]


def tick_of(role, p, c):
    if role == "F":
        return 2 - p
    if role == "O":
        return 3 * p
    return (3 - 3 * p) if c != p else -1


def tick_of_swap(role, p, c):
    if role == "F":
        return 3 - 2 * c - p
    return 1 + p if c == p else -1


def plan():
    pairs = {name: [] for name in MOVES}
    swaps = {name: [] for name in SWAPS}
    ticks = np.full((2, 2, 4, 8), -1, np.int32)
    for j in range(GRID):
        shift, p = j // 2, j % 2
        d = shift % 4
        roles = ROLES[p, d]
        for c in range(2):
            for at, name in enumerate(MOVES):
                if name in roles:
                    ticks[p, c, d, at] = tick_of(roles[name], p, c)
            for at, name in enumerate(SWAPS):
                if roles.get(name, "H") != "H":
                    ticks[p, c, d, len(MOVES) + at] = tick_of_swap(roles[name], p, c)
            for chip in range(CHIPS):
                here = (2 * chip + c) * GRID + j
                for at, name in enumerate(MOVES):
                    if ticks[p, c, d, at] < 0:
                        continue
                    role = roles[name]
                    core = 1 - c if role == "H" else c
                    if name == "relay":
                        source = chip + offset_of(role, p) - offset_of(roles["first"], p)
                    else:
                        source = chip + shift + offset_of(role, p)
                    source = (2 * (source % CHIPS) + core) * GRID + j
                    pairs[name].append((source, here))
                for at, name in enumerate(SWAPS):
                    if ticks[p, c, d, len(MOVES) + at] >= 0:
                        swaps[name].append(((2 * chip + 1 - c) * GRID + j, here))
    return pairs, swaps, ticks


def left_plan():
    skew, before, after, after2 = [], [], [], []
    wrap, wrap2 = [], []
    for i in range(GRID):
        at = lambda col: i * GRID + col % GRID
        for j in range(GRID):
            skew.append((at(i + j + 1), at(j)))
            if j > 0:
                before.append((at(j - 1), at(j)))
            if j < GRID - 1:
                after.append((at(j + 1), at(j)))
            if j < GRID - 2:
                after2.append((at(j + 1), at(j)))
        wrap += [(at(i), at(0)), (at(i + 1), at(GRID - 1))]
        wrap2 += [(at(i + 1), at(GRID - 2)), (at(i + 2), at(GRID - 1))]
    return skew, before, after, after2, wrap, wrap2


def tagged(blocks, index, count, empty):
    slots = blocks.shape[0]
    live = jnp.arange(slots, dtype=jnp.int32) < count
    first = index[0]
    second = index[1]
    if empty == 65:
        first = jnp.where(live, first, empty)
    else:
        second = jnp.where(live, second, empty)
    tag = jnp.stack([first, second]).astype(jnp.bfloat16)
    tag = jnp.pad(tag, ((0, TAG - 2), (0, BLOCK - slots)))
    return jnp.concatenate([blocks.reshape(slots * BLOCK, BLOCK), tag])


def kernel(tick_ref, *refs):
    a_refs = refs[:TICKS]
    n_b = len(MOVES) + len(SWAPS)
    b_refs = refs[TICKS : TICKS + n_b]
    out_ref, acc, tags, scal, sem = refs[TICKS + n_b :]
    for t, ref in enumerate(a_refs):
        tags[t] = ref[SA * BLOCK : SA * BLOCK + TAG, :].astype(jnp.float32)[:8].astype(jnp.int32)
    for b, ref in enumerate(b_refs):
        tags[TICKS + b] = ref[SB * BLOCK : SB * BLOCK + TAG, :].astype(jnp.float32)[:8].astype(jnp.int32)
    copy = pltpu.make_async_copy(tags, scal, sem)
    copy.start()
    acc[...] = jnp.zeros_like(acc)
    copy.wait()

    def multiply(t, b):
        a_ref, b_ref = a_refs[t], b_refs[b]

        def slot(u, carry):
            row = scal[TICKS + b, 0, u]
            hits = jnp.int32(0)
            for s in range(SA):
                hits = hits | jnp.where(scal[t, 1, s] == row, 1 << s, 0)

            @pl.when(hits != 0)
            def _():
                right = b_ref[pl.ds(pl.multiple_of(u * BLOCK, BLOCK), BLOCK), :]
                column = scal[TICKS + b, 1, u]

                def product(s, carry):
                    @pl.when((hits >> s) & 1 == 1)
                    def _():
                        left = a_ref[pl.ds(pl.multiple_of(s * BLOCK, BLOCK), BLOCK), :]
                        place = scal[t, 0, s] * KC + column
                        acc[place] += jnp.dot(left, right, preferred_element_type=jnp.float32)

                    return carry

                lax.fori_loop(0, SA, product, 0)

            return carry

        lax.fori_loop(0, SB, slot, 0)

    for b in range(n_b):
        for t in range(TICKS):
            pl.when(tick_ref[b] == t)(lambda t=t, b=b: multiply(t, b))
    for r in range(KR):
        for c in range(KC):
            out_ref[r * BLOCK : (r + 1) * BLOCK, c * BLOCK : (c + 1) * BLOCK] = acc[r * KC + c].astype(jnp.bfloat16)


def multiply_all(ticks, lefts, rights):
    n = len(lefts) + len(rights)
    return pl.pallas_call(
        kernel,
        out_shape=jax.ShapeDtypeStruct((KR * BLOCK, KC * BLOCK), jnp.bfloat16),
        in_specs=[pl.BlockSpec(memory_space=pltpu.SMEM)] + [pl.BlockSpec(memory_space=pltpu.VMEM)] * n,
        out_specs=pl.BlockSpec(memory_space=pltpu.VMEM),
        scratch_shapes=[
            pltpu.VMEM((KR * KC, BLOCK, BLOCK), jnp.float32),
            pltpu.VMEM((n, 8, BLOCK), jnp.int32),
            pltpu.SMEM((n, 8, BLOCK), jnp.int32),
            pltpu.SemaphoreType.DMA,
        ],
        compiler_params=pltpu.CompilerParams(vmem_limit_bytes=24 * 1024 * 1024),
    )(ticks, *lefts, *rights)


def local(a_blocks, a_index, a_count, b_blocks, b_index, b_count):
    row_id = lax.axis_index("row")
    col_id = lax.axis_index("col")
    pairs, swap_pairs, ticks = plan()
    ticks = jnp.asarray(ticks)[col_id % 2, row_id % 2, col_id // 2 % 4]
    left = tagged(a_blocks[0, 0], a_index[0, 0], a_count[0, 0], 64)
    right = tagged(b_blocks[0, 0, 0], b_index[0, 0, 0], b_count[0, 0, 0], 65)

    def send(value, route):
        return lax.ppermute(value, AXES, route)

    skew, before, after, after2, wrap, wrap2 = left_plan()
    moved = {"first": send(right, pairs["first"])}
    left1 = send(left, skew)
    moved["near"] = send(right, pairs["near"])
    moved["last"] = send(right, pairs["last"])
    wrapped = send(left, wrap)
    wrapped2 = send(left, wrap2)
    moved["relay"] = send(moved["first"], pairs["relay"])
    left2 = send(left1, after)
    left0 = send(left1, before)
    left2 = jnp.where(col_id == GRID - 1, wrapped, left2)
    left0 = jnp.where(col_id == 0, wrapped, left0)
    left3 = send(left2, after2)
    left3 = jnp.where(col_id >= GRID - 2, wrapped2, left3)
    swapped = [send(moved[name], swap_pairs[name]) for name in SWAPS]
    return multiply_all(ticks, (left0, left1, left2, left3), [moved[name] for name in MOVES] + swapped)


def solution(mesh):
    in_specs = (
        P("row", "col", None, None, None),
        P("row", "col", None, None),
        P("row", "col"),
        P(None, "row", "col", None, None, None),
        P(None, "row", "col", None, None),
        P(None, "row", "col"),
    )
    out_specs = P("row", "col")
    return jax.shard_map(local, mesh=mesh, in_specs=in_specs, out_specs=out_specs, check_vma=False)
```

```python
import jax
import jax.numpy as jnp
import numpy as np
from jax import lax
from jax.experimental import pallas as pl
from jax.experimental.pallas import tpu as pltpu
from jax.sharding import PartitionSpec as P

BLOCK = 128
KR = 8
KC = 4
TICKS = 4
SA = 12
SB = 6
GRID = 32
CHIPS = GRID // 2
TAG = 16
AXES = ("row", "col")

ROLES = {
    (0, 0): {"first": "F", "near": "O", "relay": "H"},
    (0, 1): {"first": "O", "near": "H", "relay": "F"},
    (0, 2): {"first": "F", "near": "H", "relay": "O"},
    (0, 3): {"first": "O", "near": "F", "relay": "H"},
    (1, 0): {"first": "F", "near": "H", "relay": "O"},
    (1, 1): {"first": "O", "near": "H", "relay": "F"},
    (1, 2): {"first": "F", "near": "O", "relay": "H"},
    (1, 3): {"first": "O", "near": "F", "relay": "H"},
}
MOVES = ("first", "near", "relay")
SWAPS = ("first", "late")
RIGHTS = len(MOVES) + len(SWAPS)
LEFTS = TICKS + 2


def offset_of(role, p):
    return {"F": 1, "O": 2 * p, "H": 2 - 2 * p}[role]


def tick_of(role, p, c):
    if role == "F":
        return 2 - p
    if role == "O":
        return 3 * p
    return (3 - 3 * p) if c != p else -1


def tick_of_swap(role, p, c):
    if role == "F":
        return 3 - 2 * c - p
    return 1 + p if c == p else -1


def plan():
    pairs = {name: [] for name in MOVES}
    swaps = {name: [] for name in SWAPS}
    ticks = np.full((2, 2, 4, 8), -1, np.int32)
    for j in range(GRID):
        shift, p = j // 2, j % 2
        d = shift % 4
        roles = ROLES[p, d]
        for c in range(2):
            for at, name in enumerate(MOVES):
                if name in roles:
                    ticks[p, c, d, at] = tick_of(roles[name], p, c)
            late = roles["near"] if roles["relay"] == "H" else roles["relay"]
            for at, role in enumerate((roles["first"], late)):
                ticks[p, c, d, len(MOVES) + at] = tick_of_swap(role, p, c)
            for chip in range(CHIPS):
                here = (2 * chip + c) * GRID + j
                for at, name in enumerate(MOVES):
                    if ticks[p, c, d, at] < 0:
                        continue
                    role = roles[name]
                    core = 1 - c if role == "H" else c
                    if name == "relay" and d != 3:
                        source = chip + offset_of(role, p) - offset_of(roles["first"], p)
                    else:
                        source = chip + shift + offset_of(role, p)
                    source = (2 * (source % CHIPS) + core) * GRID + j
                    pairs[name].append((source, here))
                for at, name in enumerate(SWAPS):
                    if ticks[p, c, d, len(MOVES) + at] >= 0:
                        swaps[name].append(((2 * chip + 1 - c) * GRID + j, here))
    table = np.full((2, GRID, 16), -1, np.int32)
    for c in range(2):
        for j in range(GRID):
            table[c, j, :8] = ticks[j % 2, c, j // 2 % 4]
            lefts = [0, 1, 2, 3, -2, -2]
            if j == 0:
                lefts[0], lefts[4] = -2, 0
            if j == GRID - 1:
                lefts[2], lefts[4] = -2, 2
            if j >= GRID - 2:
                lefts[3], lefts[5] = -2, 3
            table[c, j, 8 : 8 + LEFTS] = lefts
    return pairs, swaps, table


def left_plan():
    skew, before, after, after2 = [], [], [], []
    wrap, wrap2 = [], []
    for i in range(GRID):
        at = lambda col: i * GRID + col % GRID
        for j in range(GRID):
            skew.append((at(i + j + 1), at(j)))
            if j > 0:
                before.append((at(j - 1), at(j)))
            if j < GRID - 1:
                after.append((at(j + 1), at(j)))
            if j < GRID - 2:
                after2.append((at(j + 2), at(j)))
        wrap += [(at(i), at(0)), (at(i + 1), at(GRID - 1))]
        wrap2 += [(at(i + 1), at(GRID - 2)), (at(i + 2), at(GRID - 1))]
    return skew, before, after, after2, wrap, wrap2


def tag(index, count, empty_row, empty_column):
    slots = index.shape[1]
    live = jnp.arange(slots, dtype=jnp.int32) < count
    empty = jnp.array([[empty_row], [empty_column]], jnp.int32)
    places = jnp.where(live[None, :], index, empty).astype(jnp.bfloat16)
    return jnp.pad(places, ((0, TAG - 2), (0, BLOCK - slots)))


def join(upper, lower):
    def copy(upper_ref, lower_ref, out_ref):
        rows = upper_ref.shape[0]
        out_ref[:rows, :] = upper_ref[...]
        out_ref[rows:, :] = lower_ref[...]

    vmem = pl.BlockSpec(memory_space=pltpu.VMEM)
    size = upper.size + lower.size
    return pl.pallas_call(
        copy,
        out_shape=jax.ShapeDtypeStruct((upper.shape[0] + lower.shape[0], BLOCK), upper.dtype),
        in_specs=[vmem, vmem],
        out_specs=vmem,
        cost_estimate=pl.CostEstimate(flops=5 * 10**9, bytes_accessed=4 * size, transcendentals=0),
    )(upper, lower)


def kernel(tick_ref, *refs):
    a_refs = refs[:LEFTS]
    b_refs = refs[LEFTS : LEFTS + RIGHTS]
    out_ref, acc, tags, scal, sem = refs[LEFTS + RIGHTS :]
    for n, (ref, rows) in enumerate([(ref, SA * BLOCK) for ref in a_refs] + [(ref, SB * BLOCK) for ref in b_refs]):
        tags[n] = ref[rows : rows + TAG, :].astype(jnp.float32)[:8].astype(jnp.int32)
    copy = pltpu.make_async_copy(tags, scal, sem)
    copy.start()
    acc[...] = jnp.zeros_like(acc)
    copy.wait()

    def multiply(a, b):
        a_ref, b_ref = a_refs[a], b_refs[b]

        def slot(u, carry):
            row = scal[LEFTS + b, 0, u]
            hits = jnp.int32(0)
            for s in range(SA):
                hits = hits | jnp.where(scal[a, 1, s] == row, 1 << s, 0)

            @pl.when(hits != 0)
            def _():
                right = b_ref[pl.ds(pl.multiple_of(u * BLOCK, BLOCK), BLOCK), :]
                column = scal[LEFTS + b, 1, u]

                def product(s, carry):
                    @pl.when((hits >> s) & 1 == 1)
                    def _():
                        left = a_ref[pl.ds(pl.multiple_of(s * BLOCK, BLOCK), BLOCK), :]
                        place = scal[a, 0, s] * KC + column
                        acc[place] += jnp.dot(left, right, preferred_element_type=jnp.float32)

                    return carry

                lax.fori_loop(0, SA, product, 0)

            return carry

        lax.fori_loop(0, SB, slot, 0)

    for b in range(RIGHTS):
        for a in range(LEFTS):
            pl.when(tick_ref[b] == tick_ref[8 + a])(lambda a=a, b=b: multiply(a, b))
    for r in range(KR):
        for c in range(KC):
            out_ref[r * BLOCK : (r + 1) * BLOCK, c * BLOCK : (c + 1) * BLOCK] = acc[r * KC + c].astype(jnp.bfloat16)


def multiply_all(ticks, lefts, rights):
    n = LEFTS + RIGHTS
    return pl.pallas_call(
        kernel,
        out_shape=jax.ShapeDtypeStruct((KR * BLOCK, KC * BLOCK), jnp.bfloat16),
        in_specs=[pl.BlockSpec(memory_space=pltpu.SMEM)] + [pl.BlockSpec(memory_space=pltpu.VMEM)] * n,
        out_specs=pl.BlockSpec(memory_space=pltpu.VMEM),
        scratch_shapes=[
            pltpu.VMEM((KR * KC, BLOCK, BLOCK), jnp.float32),
            pltpu.VMEM((n, 8, BLOCK), jnp.int32),
            pltpu.SMEM((n, 8, BLOCK), jnp.int32),
            pltpu.SemaphoreType.DMA,
        ],
        compiler_params=pltpu.CompilerParams(vmem_limit_bytes=24 * 1024 * 1024),
    )(ticks, *lefts, *rights)


def send(value, route, name):
    with jax.named_scope("send_" + name):
        return lax.ppermute(value, AXES, route)


def local(a_blocks, a_index, a_count, b_blocks, b_index, b_count):
    row_id = lax.axis_index("row")
    col_id = lax.axis_index("col")
    pairs, swap_pairs, table = plan()
    ticks = jnp.asarray(table)[row_id % 2, col_id]
    skew, before, after, after2, wrap, wrap2 = left_plan()
    a_rows = a_blocks.reshape(SA * BLOCK, BLOCK)
    half = SA // 2 * BLOCK
    lower = jnp.concatenate([a_rows[half:], tag(a_index[0, 0], a_count[0, 0], 0, 64)])
    upper = a_rows[:half]
    left = jnp.concatenate([upper, lower])
    right = jnp.concatenate([b_blocks.reshape(SB * BLOCK, BLOCK), tag(b_index[0, 0, 0], b_count[0, 0, 0], 65, 0)])

    opposite = GRID * GRID // 2
    flip = lambda n: (n + opposite) % (2 * opposite)
    lower = send(lower, [(n, flip(n)) for n in range(2 * opposite)], "over")
    upper = send(upper, skew, "upper")
    lower = send(lower, [(flip(s), d) for s, d in skew], "lower")
    moved = {name: send(right, pairs[name], name) for name in MOVES[:2]}
    wrapped = send(left, wrap, "wrap")
    wrapped2 = send(left, wrap2, "wrap2")
    moved["near"], wrapped, wrapped2 = lax.optimization_barrier((moved["near"], wrapped, wrapped2))
    passing = jnp.where(col_id // 2 % 4 == 3, right, moved["first"])
    moved["relay"] = send(passing, pairs["relay"], "relay")
    swap1 = send(moved["first"], swap_pairs["first"], "swap1")
    left1 = join(upper, lower)
    left3 = send(left1, after2, "after2")
    left2 = send(left1, after, "after")
    left0 = send(left1, before, "before")
    use_near = (col_id // 2 % 4 == 3) | (col_id // 2 % 4 == 2 * (col_id % 2))
    swap2 = send(jnp.where(use_near, moved["near"], moved["relay"]), swap_pairs["late"], "swap2")
    lefts = (left0, left1, left2, left3, wrapped, wrapped2)
    return multiply_all(ticks, lefts, [moved[name] for name in MOVES] + [swap1, swap2])


def solution(mesh):
    in_specs = (
        P("row", "col", None, None, None),
        P("row", "col", None, None),
        P("row", "col"),
        P(None, "row", "col", None, None, None),
        P(None, "row", "col", None, None),
        P(None, "row", "col"),
    )
    out_specs = P("row", "col")
    return jax.shard_map(local, mesh=mesh, in_specs=in_specs, out_specs=out_specs, check_vma=False)
```

```python
import jax
import jax.numpy as jnp
import numpy as np
from jax import lax
from jax.experimental import pallas as pl
from jax.experimental.pallas import tpu as pltpu
from jax.sharding import PartitionSpec as P

BLOCK = 128
KR = 8
KC = 4
TICKS = 4
SA = 12
SB = 6
GRID = 32
CHIPS = GRID // 2
TAG = 16
AXES = ("row", "col")

ROLES = {
    (0, 0): {"first": "F", "near": "O", "relay": "H"},
    (0, 1): {"first": "O", "near": "H", "relay": "F"},
    (0, 2): {"first": "F", "near": "H", "relay": "O"},
    (0, 3): {"first": "O", "near": "F", "relay": "H"},
    (1, 0): {"first": "F", "near": "H", "relay": "O"},
    (1, 1): {"first": "O", "near": "H", "relay": "F"},
    (1, 2): {"first": "F", "near": "O", "relay": "H"},
    (1, 3): {"first": "O", "near": "F", "relay": "H"},
}
MOVES = ("first", "near", "relay")
SWAPS = ("first", "late")
RIGHTS = len(MOVES) + len(SWAPS)
LEFTS = TICKS + 2


def offset_of(role, p):
    return {"F": 1, "O": 2 * p, "H": 2 - 2 * p}[role]


def tick_of(role, p, c):
    if role == "F":
        return 2 - p
    if role == "O":
        return 3 * p
    return (3 - 3 * p) if c != p else -1


def tick_of_swap(role, p, c):
    if role == "F":
        return 3 - 2 * c - p
    return 1 + p if c == p else -1


def plan():
    pairs = {name: [] for name in MOVES}
    swaps = {name: [] for name in SWAPS}
    ticks = np.full((2, 2, 4, 8), -1, np.int32)
    for j in range(GRID):
        shift, p = j // 2, j % 2
        d = shift % 4
        roles = ROLES[p, d]
        for c in range(2):
            for at, name in enumerate(MOVES):
                if name in roles:
                    ticks[p, c, d, at] = tick_of(roles[name], p, c)
            late = roles["near"] if roles["relay"] == "H" else roles["relay"]
            for at, role in enumerate((roles["first"], late)):
                ticks[p, c, d, len(MOVES) + at] = tick_of_swap(role, p, c)
            for chip in range(CHIPS):
                here = (2 * chip + c) * GRID + j
                for at, name in enumerate(MOVES):
                    if ticks[p, c, d, at] < 0:
                        continue
                    role = roles[name]
                    core = 1 - c if role == "H" else c
                    if name == "relay" and d != 3:
                        source = chip + offset_of(role, p) - offset_of(roles["first"], p)
                    else:
                        source = chip + shift + offset_of(role, p)
                    source = (2 * (source % CHIPS) + core) * GRID + j
                    pairs[name].append((source, here))
                for at, name in enumerate(SWAPS):
                    if ticks[p, c, d, len(MOVES) + at] >= 0:
                        swaps[name].append(((2 * chip + 1 - c) * GRID + j, here))
    table = np.full((2, GRID, 16), -1, np.int32)
    for c in range(2):
        for j in range(GRID):
            table[c, j, :8] = ticks[j % 2, c, j // 2 % 4]
            lefts = [0, 1, 2, 3, -2, -2]
            if j == 0:
                lefts[0], lefts[4] = -2, 0
            if j == GRID - 1:
                lefts[2], lefts[4] = -2, 2
            if j >= GRID - 2:
                lefts[3], lefts[5] = -2, 3
            table[c, j, 8 : 8 + LEFTS] = lefts
    return pairs, swaps, table


def left_plan():
    skew, before, after, after2 = [], [], [], []
    wrap, wrap2 = [], []
    for i in range(GRID):
        at = lambda col: i * GRID + col % GRID
        for j in range(GRID):
            skew.append((at(i + j + 1), at(j)))
            if j > 0:
                before.append((at(j - 1), at(j)))
            if j < GRID - 1:
                after.append((at(j + 1), at(j)))
            if j < GRID - 2:
                after2.append((at(j + 2), at(j)))
        wrap += [(at(i), at(0)), (at(i + 1), at(GRID - 1))]
        wrap2 += [(at(i + 1), at(GRID - 2)), (at(i + 2), at(GRID - 1))]
    return skew, before, after, after2, wrap, wrap2


def tag(index, count, empty_row, empty_column):
    slots = index.shape[1]
    live = jnp.arange(slots, dtype=jnp.int32) < count
    empty = jnp.array([[empty_row], [empty_column]], jnp.int32)
    places = jnp.where(live[None, :], index, empty).astype(jnp.bfloat16)
    return jnp.pad(places, ((0, TAG - 2), (0, BLOCK - slots)))


def join(upper, lower):
    def copy(upper_ref, lower_ref, out_ref):
        rows = upper_ref.shape[0]
        out_ref[:rows, :] = upper_ref[...]
        out_ref[rows:, :] = lower_ref[...]

    vmem = pl.BlockSpec(memory_space=pltpu.VMEM)
    size = upper.size + lower.size
    return pl.pallas_call(
        copy,
        out_shape=jax.ShapeDtypeStruct((upper.shape[0] + lower.shape[0], BLOCK), upper.dtype),
        in_specs=[vmem, vmem],
        out_specs=vmem,
        cost_estimate=pl.CostEstimate(flops=5 * 10**9, bytes_accessed=4 * size, transcendentals=0),
    )(upper, lower)


def kernel(tick_ref, *refs):
    a_refs = refs[:LEFTS]
    b_refs = refs[LEFTS : LEFTS + RIGHTS]
    out_ref, acc, tags, scal, sem = refs[LEFTS + RIGHTS :]
    for n, (ref, rows) in enumerate([(ref, SA * BLOCK) for ref in a_refs] + [(ref, SB * BLOCK) for ref in b_refs]):
        tags[2 * n : 2 * n + 2, :] = ref[rows : rows + TAG, :].astype(jnp.float32)[:2].astype(jnp.int32)
    tags[2 * (LEFTS + RIGHTS) :, :] = jnp.zeros((24 - 2 * (LEFTS + RIGHTS), BLOCK), jnp.int32)
    copy = pltpu.make_async_copy(tags, scal, sem)
    copy.start()
    acc[...] = jnp.zeros_like(acc)
    copy.wait()

    def multiply(a, b):
        a_ref, b_ref = a_refs[a], b_refs[b]
        inner = [scal[2 * a + 1, s] for s in range(SA)]

        def slot(u, carry):
            row = scal[2 * (LEFTS + b), u]
            hits = jnp.int32(0)
            for s in range(SA):
                hits = hits | jnp.where(inner[s] == row, 1 << s, 0)

            @pl.when(hits != 0)
            def _():
                right = b_ref[pl.ds(pl.multiple_of(u * BLOCK, BLOCK), BLOCK), :]
                column = scal[2 * (LEFTS + b) + 1, u]

                def product(s, carry):
                    @pl.when((hits >> s) & 1 == 1)
                    def _():
                        left = a_ref[pl.ds(pl.multiple_of(s * BLOCK, BLOCK), BLOCK), :]
                        place = scal[2 * a, s] * KC + column
                        acc[place] += jnp.dot(left, right, preferred_element_type=jnp.float32)

                    return carry

                lax.fori_loop(0, SA, product, 0)

            return carry

        lax.fori_loop(0, SB, slot, 0)

    for b in range(RIGHTS):
        for a in range(LEFTS):
            pl.when(tick_ref[b] == tick_ref[8 + a])(lambda a=a, b=b: multiply(a, b))
    for r in range(KR):
        for c in range(KC):
            out_ref[r * BLOCK : (r + 1) * BLOCK, c * BLOCK : (c + 1) * BLOCK] = acc[r * KC + c].astype(jnp.bfloat16)


def multiply_all(ticks, lefts, rights):
    n = LEFTS + RIGHTS
    return pl.pallas_call(
        kernel,
        out_shape=jax.ShapeDtypeStruct((KR * BLOCK, KC * BLOCK), jnp.bfloat16),
        in_specs=[pl.BlockSpec(memory_space=pltpu.SMEM)] + [pl.BlockSpec(memory_space=pltpu.VMEM)] * n,
        out_specs=pl.BlockSpec(memory_space=pltpu.VMEM),
        scratch_shapes=[
            pltpu.VMEM((KR * KC, BLOCK, BLOCK), jnp.float32),
            pltpu.VMEM((24, BLOCK), jnp.int32),
            pltpu.SMEM((24, BLOCK), jnp.int32),
            pltpu.SemaphoreType.DMA,
        ],
        compiler_params=pltpu.CompilerParams(vmem_limit_bytes=24 * 1024 * 1024),
    )(ticks, *lefts, *rights)


def send(value, route, name):
    with jax.named_scope("send_" + name):
        return lax.ppermute(value, AXES, route)


def local(a_blocks, a_index, a_count, b_blocks, b_index, b_count):
    row_id = lax.axis_index("row")
    col_id = lax.axis_index("col")
    pairs, swap_pairs, table = plan()
    ticks = jnp.asarray(table)[row_id % 2, col_id]
    skew, before, after, after2, wrap, wrap2 = left_plan()
    a_rows = a_blocks.reshape(SA * BLOCK, BLOCK)
    half = SA // 2 * BLOCK
    lower = jnp.concatenate([a_rows[half:], tag(a_index[0, 0], a_count[0, 0], 0, 64)])
    upper = a_rows[:half]
    left = jnp.concatenate([upper, lower])
    right = jnp.concatenate([b_blocks.reshape(SB * BLOCK, BLOCK), tag(b_index[0, 0, 0], b_count[0, 0, 0], 65, 0)])

    opposite = GRID * GRID // 2
    flip = lambda n: (n + opposite) % (2 * opposite)
    lower = send(lower, [(n, flip(n)) for n in range(2 * opposite)], "over")
    upper = send(upper, skew, "upper")
    lower = send(lower, [(flip(s), d) for s, d in skew], "lower")
    moved = {name: send(right, pairs[name], name) for name in MOVES[:2]}
    wrapped = send(left, wrap, "wrap")
    wrapped2 = send(left, wrap2, "wrap2")
    moved["near"], wrapped, wrapped2 = lax.optimization_barrier((moved["near"], wrapped, wrapped2))
    passing = jnp.where(col_id // 2 % 4 == 3, right, moved["first"])
    moved["relay"] = send(passing, pairs["relay"], "relay")
    swap1 = send(moved["first"], swap_pairs["first"], "swap1")
    left1 = join(upper, lower)
    left3 = send(left1, after2, "after2")
    left2 = send(left1, after, "after")
    left0 = send(left1, before, "before")
    use_near = (col_id // 2 % 4 == 3) | (col_id // 2 % 4 == 2 * (col_id % 2))
    swap2 = send(jnp.where(use_near, moved["near"], moved["relay"]), swap_pairs["late"], "swap2")
    lefts = (left0, left1, left2, left3, wrapped, wrapped2)
    return multiply_all(ticks, lefts, [moved[name] for name in MOVES] + [swap1, swap2])


def solution(mesh):
    in_specs = (
        P("row", "col", None, None, None),
        P("row", "col", None, None),
        P("row", "col"),
        P(None, "row", "col", None, None, None),
        P(None, "row", "col", None, None),
        P(None, "row", "col"),
    )
    out_specs = P("row", "col")
    return jax.shard_map(local, mesh=mesh, in_specs=in_specs, out_specs=out_specs, check_vma=False)
```

```python
import jax
import jax.numpy as jnp
import numpy as np
from jax import lax
from jax.experimental import pallas as pl
from jax.experimental.pallas import tpu as pltpu
from jax.sharding import PartitionSpec as P

BLOCK = 128
KR = 8
KC = 4
TICKS = 4
SA = 12
SB = 6
GRID = 32
CHIPS = GRID // 2
TAG = 16
AXES = ("row", "col")

ROLES = {
    (0, 0): {"first": "F", "near": "O", "relay": "H"},
    (0, 1): {"first": "O", "near": "H", "relay": "F"},
    (0, 2): {"first": "F", "near": "H", "relay": "O"},
    (0, 3): {"first": "O", "near": "F", "relay": "H"},
    (1, 0): {"first": "F", "near": "H", "relay": "O"},
    (1, 1): {"first": "O", "near": "H", "relay": "F"},
    (1, 2): {"first": "F", "near": "O", "relay": "H"},
    (1, 3): {"first": "O", "near": "F", "relay": "H"},
}
MOVES = ("first", "near", "relay")
SWAPS = ("first", "late")
RIGHTS = len(MOVES) + len(SWAPS)
LEFTS = TICKS + 2


def offset_of(role, p):
    return {"F": 1, "O": 2 * p, "H": 2 - 2 * p}[role]


def tick_of(role, p, c):
    if role == "F":
        return 2 - p
    if role == "O":
        return 3 * p
    return (3 - 3 * p) if c != p else -1


def tick_of_swap(role, p, c):
    if role == "F":
        return 3 - 2 * c - p
    return 1 + p if c == p else -1


def plan():
    pairs = {name: [] for name in MOVES}
    swaps = {name: [] for name in SWAPS}
    ticks = np.full((2, 2, 4, 8), -1, np.int32)
    for j in range(GRID):
        shift, p = j // 2, j % 2
        d = shift % 4
        roles = ROLES[p, d]
        for c in range(2):
            for at, name in enumerate(MOVES):
                if name in roles:
                    ticks[p, c, d, at] = tick_of(roles[name], p, c)
            late = roles["near"] if roles["relay"] == "H" else roles["relay"]
            for at, role in enumerate((roles["first"], late)):
                ticks[p, c, d, len(MOVES) + at] = tick_of_swap(role, p, c)
            for chip in range(CHIPS):
                here = (2 * chip + c) * GRID + j
                for at, name in enumerate(MOVES):
                    if ticks[p, c, d, at] < 0:
                        continue
                    role = roles[name]
                    core = 1 - c if role == "H" else c
                    if name == "relay" and d != 3:
                        source = chip + offset_of(role, p) - offset_of(roles["first"], p)
                    else:
                        source = chip + shift + offset_of(role, p)
                    source = (2 * (source % CHIPS) + core) * GRID + j
                    pairs[name].append((source, here))
                for at, name in enumerate(SWAPS):
                    if ticks[p, c, d, len(MOVES) + at] >= 0:
                        swaps[name].append(((2 * chip + 1 - c) * GRID + j, here))
    table = np.full((2, GRID, 16), -1, np.int32)
    for c in range(2):
        for j in range(GRID):
            table[c, j, :8] = ticks[j % 2, c, j // 2 % 4]
            lefts = [0, 1, 2, 3, -2, -2]
            if j == 0:
                lefts[0], lefts[4] = -2, 0
            if j == GRID - 1:
                lefts[2], lefts[4] = -2, 2
            if j >= GRID - 2:
                lefts[3], lefts[5] = -2, 3
            table[c, j, 8 : 8 + LEFTS] = lefts
    return pairs, swaps, table


def left_plan():
    skew, before, after, after2 = [], [], [], []
    wrap, wrap2 = [], []
    for i in range(GRID):
        at = lambda col: i * GRID + col % GRID
        for j in range(GRID):
            skew.append((at(i + j + 1), at(j)))
            if j > 0:
                before.append((at(j - 1), at(j)))
            if j < GRID - 1:
                after.append((at(j + 1), at(j)))
            if j < GRID - 2:
                after2.append((at(j + 2), at(j)))
        wrap += [(at(i), at(0)), (at(i + 1), at(GRID - 1))]
        wrap2 += [(at(i + 1), at(GRID - 2)), (at(i + 2), at(GRID - 1))]
    return skew, before, after, after2, wrap, wrap2


def tag(index, count, empty_row, empty_column):
    slots = index.shape[1]
    live = jnp.arange(slots, dtype=jnp.int32) < count
    empty = jnp.array([[empty_row], [empty_column]], jnp.int32)
    places = jnp.where(live[None, :], index, empty).astype(jnp.bfloat16)
    return jnp.pad(places, ((0, TAG - 2), (0, BLOCK - slots)))


def kernel(tick_ref, *refs):
    a_refs = refs[:LEFTS]
    b_refs = refs[LEFTS : LEFTS + RIGHTS]
    out_ref, acc, tags, scal, sem = refs[LEFTS + RIGHTS :]
    for n, (ref, rows) in enumerate([(ref, SA * BLOCK) for ref in a_refs] + [(ref, SB * BLOCK) for ref in b_refs]):
        tags[2 * n : 2 * n + 2, :] = ref[rows : rows + TAG, :].astype(jnp.float32)[:2].astype(jnp.int32)
    tags[2 * (LEFTS + RIGHTS) :, :] = jnp.zeros((24 - 2 * (LEFTS + RIGHTS), BLOCK), jnp.int32)
    copy = pltpu.make_async_copy(tags, scal, sem)
    copy.start()
    acc[...] = jnp.zeros_like(acc)
    copy.wait()

    def multiply(a, b):
        a_ref, b_ref = a_refs[a], b_refs[b]
        inner = [scal[2 * a + 1, s] for s in range(SA)]

        def slot(u, carry):
            row = scal[2 * (LEFTS + b), u]
            hits = jnp.int32(0)
            for s in range(SA):
                hits = hits | jnp.where(inner[s] == row, 1 << s, 0)

            @pl.when(hits != 0)
            def _():
                right = b_ref[pl.ds(pl.multiple_of(u * BLOCK, BLOCK), BLOCK), :]
                column = scal[2 * (LEFTS + b) + 1, u]

                def product(s, carry):
                    @pl.when((hits >> s) & 1 == 1)
                    def _():
                        left = a_ref[pl.ds(pl.multiple_of(s * BLOCK, BLOCK), BLOCK), :]
                        place = scal[2 * a, s] * KC + column
                        acc[place] += jnp.dot(left, right, preferred_element_type=jnp.float32)

                    return carry

                lax.fori_loop(0, SA, product, 0)

            return carry

        lax.fori_loop(0, SB, slot, 0)

    for b in range(RIGHTS):
        for a in range(LEFTS):
            pl.when(tick_ref[b] == tick_ref[8 + a])(lambda a=a, b=b: multiply(a, b))
    for r in range(KR):
        for c in range(KC):
            out_ref[r * BLOCK : (r + 1) * BLOCK, c * BLOCK : (c + 1) * BLOCK] = acc[r * KC + c].astype(jnp.bfloat16)


def multiply_all(ticks, lefts, rights):
    n = LEFTS + RIGHTS
    return pl.pallas_call(
        kernel,
        out_shape=jax.ShapeDtypeStruct((KR * BLOCK, KC * BLOCK), jnp.bfloat16),
        in_specs=[pl.BlockSpec(memory_space=pltpu.SMEM)] + [pl.BlockSpec(memory_space=pltpu.VMEM)] * n,
        out_specs=pl.BlockSpec(memory_space=pltpu.VMEM),
        scratch_shapes=[
            pltpu.VMEM((KR * KC, BLOCK, BLOCK), jnp.float32),
            pltpu.VMEM((24, BLOCK), jnp.int32),
            pltpu.SMEM((24, BLOCK), jnp.int32),
            pltpu.SemaphoreType.DMA,
        ],
        compiler_params=pltpu.CompilerParams(vmem_limit_bytes=24 * 1024 * 1024),
    )(ticks, *lefts, *rights)


def send(value, route, name):
    with jax.named_scope("send_" + name):
        return lax.ppermute(value, AXES, route)


def local(a_blocks, a_index, a_count, b_blocks, b_index, b_count):
    row_id = lax.axis_index("row")
    col_id = lax.axis_index("col")
    pairs, swap_pairs, table = plan()
    ticks = jnp.asarray(table)[row_id % 2, col_id]
    skew, before, after, after2, wrap, wrap2 = left_plan()
    a_rows = a_blocks.reshape(SA * BLOCK, BLOCK)
    half = SA // 2 * BLOCK
    lower = jnp.concatenate([a_rows[half:], tag(a_index[0, 0], a_count[0, 0], 0, 64)])
    upper = a_rows[:half]
    left = jnp.concatenate([upper, lower])
    right = jnp.concatenate([b_blocks.reshape(SB * BLOCK, BLOCK), tag(b_index[0, 0, 0], b_count[0, 0, 0], 65, 0)])

    opposite = GRID * GRID // 2
    flip = lambda n: (n + opposite) % (2 * opposite)
    lower = send(lower, [(n, flip(n)) for n in range(2 * opposite)], "over")
    upper = send(upper, skew, "upper")
    lower = send(lower, [(flip(s), d) for s, d in skew], "lower")
    moved = {name: send(right, pairs[name], name) for name in MOVES[:2]}
    wrapped = send(left, wrap, "wrap")
    wrapped2 = send(left, wrap2, "wrap2")
    moved["near"], wrapped, wrapped2 = lax.optimization_barrier((moved["near"], wrapped, wrapped2))
    passing = jnp.where(col_id // 2 % 4 == 3, right, moved["first"])
    moved["relay"] = send(passing, pairs["relay"], "relay")
    swap1 = send(moved["first"], swap_pairs["first"], "swap1")
    left1 = jnp.concatenate([upper, lower])
    left3 = send(left1, after2, "after2")
    left2 = send(left1, after, "after")
    left0 = send(left1, before, "before")
    use_near = (col_id // 2 % 4 == 3) | (col_id // 2 % 4 == 2 * (col_id % 2))
    swap2 = send(jnp.where(use_near, moved["near"], moved["relay"]), swap_pairs["late"], "swap2")
    lefts = (left0, left1, left2, left3, wrapped, wrapped2)
    return multiply_all(ticks, lefts, [moved[name] for name in MOVES] + [swap1, swap2])


def solution(mesh):
    in_specs = (
        P("row", "col", None, None, None),
        P("row", "col", None, None),
        P("row", "col"),
        P(None, "row", "col", None, None, None),
        P(None, "row", "col", None, None),
        P(None, "row", "col"),
    )
    out_specs = P("row", "col")
    return jax.shard_map(local, mesh=mesh, in_specs=in_specs, out_specs=out_specs, check_vma=False)
```
